32 devices in a mesh: groups: 2 (over x), section: 8 (over z, y), rows: 2 (over core).
Axes of the slice: x: 2, y: 2, z: 4, core: 2. Of those that a mesh axis runs over, the one named last changes fastest.
Arguments:
- inputs: bfloat16 [8, 16, 64, 256], P('groups', 'rows'), parts along dimension 0, may hold values from -6 to 6
- weights: bfloat16 [8, 2304, 256], P('section'), may hold values from -0.1875 to 0.1875
- cotangent: bfloat16 [8, 16, 64, 256], P('groups', 'rows'), parts along dimension 0, may hold values from -6 to 6
Outputs:
- section_outputs: bfloat16 [8, 8, 16, 64, 256], P('section', 'groups', 'rows'), parts along dimension 1
- grad_inputs: bfloat16 [8, 8, 16, 64, 256], P('section', 'groups', 'rows'), parts along dimension 1
- weight_grads: float32 [8, 4608, 256], P('section', 'groups'), parts along dimension 1
The draws below stay inside these ranges and needn't reach their ends.
There are 2 independent parts, one for each index of `groups`. The reference program is written for one: setup_inputs(seed, part) draws one part's arguments, and reference() takes and returns one part's arrays. A program takes and returns all parts, laid end to end along the dimension named above; an argument that names none is the same for every part. Nothing has to cross between parts.
All inputs are finite; a program needn't handle non-finite values.
Results may differ from the reference program's by a relative error of at most 0.028.
Values may be sent and summed in bfloat16 or wider, within the bound.
A program may use at most 64 MiB of HBM per device.

```python
import math
import jax
import jax.numpy as jnp

C = 256
WD = 64
MICRO = 4
SECTIONS = 8
H = 16


def block_levels(rng, shape, pieces, low, top_value):
    level = 1.0
    for position, parts in pieces:
        heights = jax.random.uniform(jax.random.fold_in(jax.random.fold_in(rng, 6), position), (parts,), jnp.float32, low / len(pieces), top_value / len(pieces))
        level = level * jnp.repeat(jnp.exp(heights), shape[position] // parts).reshape((-1,) + (1,) * (len(shape) - 1 - position))
    return level


def normal_values(key, dims, spread, bound, split=(), held_as=jnp.bfloat16):
    factor_of = block_levels(key, dims, split, -0.22, 0.18) if split else 1.0
    array = jax.random.normal(key, dims, jnp.float32) * spread * factor_of
    return jnp.minimum(jnp.maximum(array, -bound), bound).astype(held_as)


def setup_inputs(seed: int = 0, part: int = 0) -> dict:
    key_list = jax.random.split(jax.random.key(seed), 4)
    part_splits = jax.random.split(jax.random.fold_in(key_list[3], part), 4)
    return {
        "inputs": normal_values(part_splits[0], (MICRO, H, WD, C), 1.0, 6.0, ((1, 2),)),
        "weights": normal_values(key_list[1], (SECTIONS, 9 * C, C), (9 * C // 2) ** -0.5, 0.1875, ((0, 8),)),
        "cotangent": normal_values(part_splits[2], (MICRO, H, WD, C), 1.0, 6.0, ((1, 2),)),
    }


tanh_scale = 0.7978845608028654
cubic_term = 0.044715

def gelu_value(values):
    curved = jnp.tanh(tanh_scale * (values + cubic_term * values * values * values))
    return 0.5 * values * (1.0 + curved)

def gelu_slope(values):
    curved = jnp.tanh(tanh_scale * (values + cubic_term * values * values * values))
    return 0.5 * (1.0 + curved) + 0.5 * values * (1.0 - curved * curved) * tanh_scale * (1.0 + 3.0 * cubic_term * values * values)

def window(padded, row_count, col_count):
    return jnp.concatenate([padded[row_off:row_off + row_count, col_off:col_off + col_count] for row_off in range(3) for col_off in range(3)], axis=-1)

def flipped(padded, row_count, col_count):
    return jnp.concatenate([padded[2 - row_off:2 - row_off + row_count, 2 - col_off:2 - col_off + col_count] for row_off in range(3) for col_off in range(3)], axis=-1)

def reference(inputs, weights, cotangent):
    height = inputs.shape[1]
    col_count = inputs.shape[2]
    channels = inputs.shape[3]
    pixels = height * col_count
    totals = [jnp.zeros((9 * channels, channels), jnp.float32) for section_num in range(SECTIONS)]
    outputs_all = []
    grads_all = []
    for micro_num in range(MICRO):
        current = inputs[micro_num]
        framed_list = []
        preact_list = []
        outputs_list = []
        for section_num in range(SECTIONS):
            framed = jnp.pad(current, ((1, 1), (1, 1), (0, 0)))
            preact = jnp.dot(window(framed, height, col_count).reshape(pixels, 9 * channels), weights[section_num], preferred_element_type=jnp.float32).reshape(height, col_count, channels)
            current = gelu_value(preact).astype(jnp.bfloat16)
            framed_list.append(framed)
            preact_list.append(preact)
            outputs_list.append(current)
        upstream = cotangent[micro_num]
        grads_list = [None] * SECTIONS
        for section_num in range(SECTIONS - 1, -1, -1):
            local_grad = (upstream.astype(jnp.float32) * gelu_slope(preact_list[section_num])).astype(jnp.bfloat16)
            transposed = weights[section_num].reshape(9, channels, channels).transpose(0, 2, 1).reshape(9 * channels, channels)
            padded_grad = jnp.pad(local_grad, ((1, 1), (1, 1), (0, 0)))
            upstream = jnp.dot(flipped(padded_grad, height, col_count).reshape(pixels, 9 * channels), transposed, preferred_element_type=jnp.float32).reshape(height, col_count, channels).astype(jnp.bfloat16)
            grads_list[section_num] = upstream
            columns = window(framed_list[section_num], height, col_count).reshape(pixels, 9 * channels)
            totals[section_num] = totals[section_num] + jnp.dot(columns.T, local_grad.reshape(pixels, channels), preferred_element_type=jnp.float32)
        outputs_all.append(outputs_list)
        grads_all.append(grads_list)
    section_outputs = jnp.stack([jnp.stack([outputs_all[micro_num][section_num] for micro_num in range(MICRO)]) for section_num in range(SECTIONS)])
    grad_inputs = jnp.stack([jnp.stack([grads_all[micro_num][section_num] for micro_num in range(MICRO)]) for section_num in range(SECTIONS)])
    factor = 1.0 / math.sqrt(MICRO * pixels)
    weight_grads = jnp.stack(totals) * factor
    return (section_outputs, grad_inputs, weight_grads)
```

```python
import functools
import math

import jax
import jax.numpy as jnp
from jax import lax
from jax.experimental import pallas as pl
from jax.experimental.pallas import tpu as pltpu
from jax.sharding import PartitionSpec as P

MESH = pl.DeviceIdType.MESH
tanh_scale = 0.7978845608028654
cubic_term = 0.044715


def column_shifts(values):
    rows, cols, channels = values.shape
    flat = values.reshape(rows * cols, channels)
    col = lax.broadcasted_iota(jnp.int32, flat.shape, 0) % cols
    left = jnp.where(col == 0, 0.0, pltpu.roll(flat, 1, 0))
    right = jnp.where(col == cols - 1, 0.0, pltpu.roll(flat, rows * cols - 1, 0))
    return (
        left.astype(jnp.bfloat16).reshape(values.shape),
        right.astype(jnp.bfloat16).reshape(values.shape),
    )


def kernel(
    section_count,
    factor,
    in_ref,
    w_ref,
    cot_ref,
    out_ref,
    grad_ref,
    wgrad_ref,
    x3,
    u,
    slope,
    g3,
    wt,
    acc,
    wsend,
    wrecv,
    send_f,
    recv_f,
    send_b,
    recv_b,
    send_i,
    send_c,
    send_s,
    recv_s,
    send_w,
    recv_w,
):
    micros, rows, cols, chans = in_ref.shape
    half = rows // 2
    mid = pl.ds(chans, chans)
    s = lax.axis_index("section")
    r = lax.axis_index("rows")
    other = 1 - r
    last = section_count - 1
    is_first = s == 0
    is_last = s == last

    edge = (1 - r) * (rows - 1)
    halo = (1 - r) * (rows + 1)
    other_halo = r * (rows + 1)

    barrier = pltpu.get_barrier_semaphore()
    pl.semaphore_signal(barrier, inc=1, device_id={"rows": other}, device_id_type=MESH)

    @pl.when(s > 0)
    def _():
        for core in range(2):
            pl.semaphore_signal(
                barrier, inc=1, device_id={"section": s - 1, "rows": core}, device_id_type=MESH
            )

    @pl.when(s < last)
    def _():
        for core in range(2):
            pl.semaphore_signal(
                barrier, inc=1, device_id={"section": s + 1, "rows": core}, device_id_type=MESH
            )

    peers = 1 + 2 * (s > 0).astype(jnp.int32) + 2 * (s < last).astype(jnp.int32)
    pl.semaphore_wait(barrier, peers)

    def first_halo(m, dst_row):
        return pltpu.make_async_remote_copy(
            src_ref=in_ref.at[m, pl.ds(edge, 1)],
            dst_ref=x3.at[m, pl.ds(dst_row, 1), :, mid],
            send_sem=send_i.at[m],
            recv_sem=recv_f.at[m, 2],
            device_id={"rows": other},
            device_id_type=MESH,
        )

    def last_halo(m, dst_row):
        return pltpu.make_async_remote_copy(
            src_ref=cot_ref.at[m, pl.ds(edge, 1)],
            dst_ref=u.at[m, pl.ds(dst_row, 1)],
            send_sem=send_c.at[m],
            recv_sem=recv_b.at[m, 2],
            device_id={"rows": other},
            device_id_type=MESH,
        )

    def slope_halo(m, dst_row):
        return pltpu.make_async_remote_copy(
            src_ref=slope.at[m, pl.ds(edge + 1, 1)],
            dst_ref=slope.at[m, pl.ds(dst_row, 1)],
            send_sem=send_s.at[m],
            recv_sem=recv_s.at[m],
            device_id={"rows": other},
            device_id_type=MESH,
        )

    starts = (r * half, half - r, edge, (1 - r) * (half + 1))
    counts = (half, 1, 1, half - 1)

    def forward_piece(m, p, halo_row):
        start, count = starts[p], counts[p]
        where = halo_row if p == 2 else start + 1
        return pltpu.make_async_remote_copy(
            src_ref=out_ref.at[m, pl.ds(start, count)],
            dst_ref=x3.at[m, pl.ds(where, count), :, mid],
            send_sem=send_f.at[m, p],
            recv_sem=recv_f.at[m, p],
            device_id={"section": jnp.minimum(s + 1, last), "rows": other if p == 2 else r},
            device_id_type=MESH,
        )

    def backward_piece(m, p, halo_row):
        start, count = starts[p], counts[p]
        where = halo_row if p == 2 else start + 1
        return pltpu.make_async_remote_copy(
            src_ref=grad_ref.at[m, pl.ds(start, count)],
            dst_ref=u.at[m, pl.ds(where, count)],
            send_sem=send_b.at[m, p],
            recv_sem=recv_b.at[m, p],
            device_id={"section": jnp.maximum(s - 1, 0), "rows": other if p == 2 else r},
            device_id_type=MESH,
        )

    @pl.when(is_first)
    def _():
        def start(m, carry):
            first_halo(m, other_halo).start()
            return carry

        lax.fori_loop(0, micros, start, 0)

    @pl.when(is_last)
    def _():
        def start(m, carry):
            last_halo(m, other_halo).start()
            u[m, pl.ds(1, rows)] = cot_ref[m]
            return carry

        lax.fori_loop(0, micros, start, 0)

    blank = jnp.zeros((1, cols, 3 * chans), jnp.bfloat16)

    def clear(m, carry):
        x3[m, pl.ds(other_halo, 1)] = blank
        return carry

    lax.fori_loop(0, micros, clear, 0)
    g3[pl.ds(other_halo, 1)] = blank

    def transpose_weights():
        for k in range(9):
            wt[pl.ds((8 - k) * chans, chans), :] = w_ref[pl.ds(k * chans, chans), :].T

    @pl.when(s > 0)
    def _():
        transpose_weights()

    new_starts = (1 + r * (half - 1), (1 - r) * (half + 2))
    new_counts = (half + 1, rows - half)
    half_starts = (r * half, (1 - r) * half)

    def conv(field, kern, start):
        total = None
        for a in range(3):
            part = jnp.dot(
                field[pl.ds(start + a, half)].reshape(half * cols, 3 * chans),
                kern[pl.ds(a * 3 * chans, 3 * chans), :],
                preferred_element_type=jnp.float32,
            )
            total = part if total is None else total + part
        return total

    def forward(m):
        @pl.when(is_first)
        def _():
            x3[m, pl.ds(1, rows), :, mid] = in_ref[m]

        for k in range(2):
            @pl.when(s > 0)
            def _():
                for p in ((0, 1), (3,))[k]:
                    forward_piece(m, p, halo).wait_recv()

            if k == 1:
                forward_piece(m, 2, halo).wait_recv()
            fresh = pl.ds(new_starts[k], new_counts[k])
            left, right = column_shifts(x3[m, fresh, :, mid].astype(jnp.float32))
            x3[m, fresh, :, pl.ds(0, chans)] = left
            x3[m, fresh, :, pl.ds(2 * chans, chans)] = right
            start = half_starts[k]
            pre = conv(x3.at[m], w_ref, start)
            curved = jnp.tanh(tanh_scale * (pre + cubic_term * pre * pre * pre))
            value = 0.5 * pre * (1.0 + curved)
            out_ref[m, pl.ds(start, half)] = value.astype(jnp.bfloat16).reshape(half, cols, chans)

            @pl.when(s < last)
            def _():
                for p in ((0,), (1, 2, 3))[k]:
                    forward_piece(m, p, other_halo).start()

            steep = 0.5 * (1.0 + curved) + 0.5 * pre * (1.0 - curved * curved) * tanh_scale * (
                1.0 + 3.0 * cubic_term * pre * pre
            )
            slope[m, pl.ds(start + 1, half)] = steep.reshape(half, cols, chans)
        slope_halo(m, other_halo).start()

    def kernel_term(m, a):
        return lax.dot_general(
            x3[m, pl.ds(a, rows)].reshape(rows * cols, 3 * chans),
            g3[pl.ds(1, rows), :, mid].reshape(rows * cols, chans),
            (((0,), (0,)), ((), ())),
            preferred_element_type=jnp.float32,
        )

    def backward(m):
        for k in range(2):
            @pl.when(s < last)
            def _():
                for p in ((0, 1), (3,))[k]:
                    backward_piece(m, p, halo).wait_recv()

            if k == 1:
                backward_piece(m, 2, halo).wait_recv()
                slope_halo(m, halo).wait_recv()
            fresh = pl.ds(new_starts[k], new_counts[k])
            local = (u[m, fresh].astype(jnp.float32) * slope[m, fresh]).astype(jnp.bfloat16)
            left, right = column_shifts(local.astype(jnp.float32))
            g3[fresh, :, pl.ds(0, chans)] = left
            g3[fresh, :, mid] = local
            g3[fresh, :, pl.ds(2 * chans, chans)] = right
            start = half_starts[k]
            passed = conv(g3, wt, start)
            grad_ref[m, pl.ds(start, half)] = passed.astype(jnp.bfloat16).reshape(half, cols, chans)

            @pl.when(s > 0)
            def _():
                for p in ((0,), (1, 2, 3))[k]:
                    backward_piece(m, p, other_halo).start()

        @pl.when(m == 0)
        def _():
            for a in range(3):
                acc[pl.ds(a * 3 * chans, 3 * chans), :] = kernel_term(m, a)

        @pl.when(jnp.logical_and(m > 0, m < micros - 1))
        def _():
            for a in range(3):
                acc[pl.ds(a * 3 * chans, 3 * chans), :] += kernel_term(m, a)

    def forward_step(m, carry):
        forward(m)

        @pl.when(is_last)
        def _():
            backward(m)

        return carry

    lax.fori_loop(0, micros, forward_step, 0)

    @pl.when(s == 0)
    def _():
        transpose_weights()

    def backward_step(m, carry):
        backward(m)
        return carry

    @pl.when(s < last)
    def _():
        lax.fori_loop(0, micros, backward_step, 0)

    def kernel_copy(a):
        block = pl.ds(a * 3 * chans, 3 * chans)
        return pltpu.make_async_remote_copy(
            src_ref=wsend.at[block],
            dst_ref=wrecv.at[block],
            send_sem=send_w.at[a],
            recv_sem=recv_w.at[a],
            device_id={"rows": other},
            device_id_type=MESH,
        )

    for a in range(3):
        block = pl.ds(a * 3 * chans, 3 * chans)
        term = kernel_term(micros - 1, a)
        total = term if micros == 1 else acc[block, :] + term
        wsend[block, :] = total.astype(jnp.bfloat16)
        kernel_copy(a).start()
    for a in range(3):
        block = pl.ds(a * 3 * chans, 3 * chans)
        kernel_copy(a).wait_recv()
        wgrad_ref[block, :] = (
            wsend[block, :].astype(jnp.float32) + wrecv[block, :].astype(jnp.float32)
        ) * factor

    def finish(m, carry):
        slope_halo(m, other_halo).wait_send()

        @pl.when(s < last)
        def _():
            for p in range(4):
                forward_piece(m, p, other_halo).wait_send()

        @pl.when(s > 0)
        def _():
            for p in range(4):
                backward_piece(m, p, other_halo).wait_send()

        @pl.when(is_first)
        def _():
            first_halo(m, other_halo).wait_send()

        @pl.when(is_last)
        def _():
            last_halo(m, other_halo).wait_send()

        return carry

    lax.fori_loop(0, micros, finish, 0)
    for a in range(3):
        kernel_copy(a).wait_send()


def on_device(inputs, weights, cotangent):
    micros, rows, cols, chans = inputs.shape
    depth = weights.shape[1]
    section_count = lax.axis_size("section")
    factor = 1.0 / math.sqrt(micros * rows * lax.axis_size("rows") * cols)
    vmem = pl.BlockSpec(memory_space=pltpu.VMEM)
    dma = pltpu.SemaphoreType.DMA
    bf16, f32 = jnp.bfloat16, jnp.float32
    outs = pl.pallas_call(
        functools.partial(kernel, section_count, factor),
        out_shape=(
            jax.ShapeDtypeStruct((micros, rows, cols, chans), bf16),
            jax.ShapeDtypeStruct((micros, rows, cols, chans), bf16),
            jax.ShapeDtypeStruct((depth, chans), f32),
        ),
        in_specs=[vmem] * 3,
        out_specs=(vmem,) * 3,
        scratch_shapes=[
            pltpu.VMEM((micros, rows + 2, cols, 3 * chans), bf16),
            pltpu.VMEM((micros, rows + 2, cols, chans), bf16),
            pltpu.VMEM((micros, rows + 2, cols, chans), f32),
            pltpu.VMEM((rows + 2, cols, 3 * chans), bf16),
            pltpu.VMEM((depth, chans), bf16),
            pltpu.VMEM((depth, chans), f32),
            pltpu.VMEM((depth, chans), bf16),
            pltpu.VMEM((depth, chans), bf16),
            dma((micros, 4)),
            dma((micros, 4)),
            dma((micros, 4)),
            dma((micros, 4)),
            dma((micros,)),
            dma((micros,)),
            dma((micros,)),
            dma((micros,)),
            dma((3,)),
            dma((3,)),
        ],
        compiler_params=pltpu.CompilerParams(
            collective_id=0, has_side_effects=True, vmem_limit_bytes=48 * 1024 * 1024
        ),
        name="relay",
    )(inputs, weights[0], cotangent)
    section_outputs, grad_inputs, weight_grads = outs
    return (section_outputs[None], grad_inputs[None], weight_grads[None])


def solution(mesh):
    placed = (
        P("groups", "rows", None, None),
        P("section", None, None),
        P("groups", "rows", None, None),
    )
    return jax.shard_map(
        on_device,
        mesh=mesh,
        in_specs=placed,
        out_specs=(
            P("section", "groups", "rows", None, None),
            P("section", "groups", "rows", None, None),
            P("section", "groups", None),
        ),
        check_vma=False,
    )
```

```python
import functools
import math

import jax
import jax.numpy as jnp
from jax import lax
from jax.experimental import pallas as pl
from jax.experimental.pallas import tpu as pltpu
from jax.sharding import PartitionSpec as P

MESH = pl.DeviceIdType.MESH
tanh_scale = 0.7978845608028654
cubic_term = 0.044715
PARTS = 4


def column_shifts(values):
    rows, cols, channels = values.shape
    flat = values.reshape(rows * cols, channels)
    col = lax.broadcasted_iota(jnp.int32, flat.shape, 0) % cols
    left = jnp.where(col == 0, 0.0, pltpu.roll(flat, 1, 0))
    right = jnp.where(col == cols - 1, 0.0, pltpu.roll(flat, rows * cols - 1, 0))
    return (
        left.astype(jnp.bfloat16).reshape(values.shape),
        right.astype(jnp.bfloat16).reshape(values.shape),
    )


def kernel(
    section_count,
    factor,
    in_ref,
    w_hbm,
    cot_ref,
    out_ref,
    grad_ref,
    wgrad_ref,
    w_ref,
    x3,
    u,
    slope,
    g3,
    wt,
    acc,
    wsend,
    wrecv,
    send_f,
    recv_f,
    send_b,
    recv_b,
    send_i,
    send_c,
    send_s,
    recv_s,
    send_w,
    recv_w,
    sem_in,
    sem_wt,
):
    micros, rows, cols, chans = in_ref.shape
    step = rows // PARTS
    last_part = PARTS - 1
    mid = pl.ds(chans, chans)
    s = lax.axis_index("section")
    r = lax.axis_index("rows")
    other = 1 - r
    last = section_count - 1
    is_first = s == 0
    is_last = s == last

    edge = (1 - r) * (rows - 1)
    halo = (1 - r) * (rows + 1)
    other_halo = r * (rows + 1)

    weight_copy = pltpu.make_async_copy(w_hbm, w_ref, sem_wt)
    weight_copy.start()

    def own_input(m):
        return pltpu.make_async_copy(in_ref.at[m], x3.at[m, pl.ds(1, rows), :, mid], sem_in.at[m])

    def own_cotangent(m):
        return pltpu.make_async_copy(cot_ref.at[m], u.at[m, pl.ds(1, rows)], sem_in.at[m])

    def each_micro(action):
        def body(m, carry):
            action(m)
            return carry

        lax.fori_loop(0, micros, body, 0)

    @pl.when(is_first)
    def _():
        each_micro(lambda m: own_input(m).start())

    @pl.when(is_last)
    def _():
        each_micro(lambda m: own_cotangent(m).start())

    barrier = pltpu.get_barrier_semaphore()
    pl.semaphore_signal(barrier, inc=1, device_id={"rows": other}, device_id_type=MESH)

    @pl.when(s > 0)
    def _():
        for core in range(2):
            pl.semaphore_signal(
                barrier, inc=1, device_id={"section": s - 1, "rows": core}, device_id_type=MESH
            )

    @pl.when(s < last)
    def _():
        for core in range(2):
            pl.semaphore_signal(
                barrier, inc=1, device_id={"section": s + 1, "rows": core}, device_id_type=MESH
            )

    peers = 1 + 2 * (s > 0).astype(jnp.int32) + 2 * (s < last).astype(jnp.int32)
    pl.semaphore_wait(barrier, peers)

    def first_halo(m, dst_row):
        return pltpu.make_async_remote_copy(
            src_ref=in_ref.at[m, pl.ds(edge, 1)],
            dst_ref=x3.at[m, pl.ds(dst_row, 1), :, mid],
            send_sem=send_i.at[m],
            recv_sem=recv_f.at[m, 2 * PARTS - 1],
            device_id={"rows": other},
            device_id_type=MESH,
        )

    def last_halo(m, dst_row):
        return pltpu.make_async_remote_copy(
            src_ref=cot_ref.at[m, pl.ds(edge, 1)],
            dst_ref=u.at[m, pl.ds(dst_row, 1)],
            send_sem=send_c.at[m],
            recv_sem=recv_b.at[m, 2 * PARTS - 1],
            device_id={"rows": other},
            device_id_type=MESH,
        )

    def slope_halo(m, dst_row):
        return pltpu.make_async_remote_copy(
            src_ref=slope.at[m, pl.ds(edge + 1, 1)],
            dst_ref=slope.at[m, pl.ds(dst_row, 1)],
            send_sem=send_s.at[m],
            recv_sem=recv_s.at[m],
            device_id={"rows": other},
            device_id_type=MESH,
        )

    def run_start(q, n):
        return q + r * (rows - 2 * q - n)

    pieces = [(0, step)]
    pieces += [(k * step + 1, step - 1) for k in range(1, PARTS)]
    pieces += [(k * step, 1) for k in range(1, PARTS)]
    pieces += [(rows - 1, 1)]
    middle = 2 * PARTS - 1
    needs = [(k, PARTS + k if k < last_part else middle) for k in range(PARTS)]
    gives = [(0,)] + [(PARTS - 1 + k, k) for k in range(1, last_part)]
    gives += [(PARTS - 1 + last_part, middle, last_part)]

    def forward_piece(m, p, halo_row):
        q, count = pieces[p]
        start = run_start(q, count)
        where = halo_row if p == middle else start + 1
        return pltpu.make_async_remote_copy(
            src_ref=out_ref.at[m, pl.ds(start, count)],
            dst_ref=x3.at[m, pl.ds(where, count), :, mid],
            send_sem=send_f.at[m, p],
            recv_sem=recv_f.at[m, p],
            device_id={"section": jnp.minimum(s + 1, last), "rows": other if p == middle else r},
            device_id_type=MESH,
        )

    def backward_piece(m, p, halo_row):
        q, count = pieces[p]
        start = run_start(q, count)
        where = halo_row if p == middle else start + 1
        return pltpu.make_async_remote_copy(
            src_ref=grad_ref.at[m, pl.ds(start, count)],
            dst_ref=u.at[m, pl.ds(where, count)],
            send_sem=send_b.at[m, p],
            recv_sem=recv_b.at[m, p],
            device_id={"section": jnp.maximum(s - 1, 0), "rows": other if p == middle else r},
            device_id_type=MESH,
        )

    @pl.when(is_first)
    def _():
        each_micro(lambda m: first_halo(m, other_halo).start())

    @pl.when(is_last)
    def _():
        each_micro(lambda m: last_halo(m, other_halo).start())

    blank = jnp.zeros((1, cols, 3 * chans), jnp.bfloat16)

    def clear(m, carry):
        x3[m, pl.ds(other_halo, 1)] = blank
        return carry

    lax.fori_loop(0, micros, clear, 0)
    g3[pl.ds(other_halo, 1)] = blank

    weight_copy.wait()

    def transpose_weights():
        for k in range(9):
            wt[pl.ds((8 - k) * chans, chans), :] = w_ref[pl.ds(k * chans, chans), :].T

    @pl.when(s > 0)
    def _():
        transpose_weights()

    fresh_runs = [(0, step + 1)] + [(k * step + 1, step) for k in range(1, PARTS)]

    def conv(field, kern, start):
        total = None
        for a in range(3):
            part = jnp.dot(
                field[pl.ds(start + a, step)].reshape(step * cols, 3 * chans),
                kern[pl.ds(a * 3 * chans, 3 * chans), :],
                preferred_element_type=jnp.float32,
            )
            total = part if total is None else total + part
        return total

    def forward(m):
        @pl.when(is_first)
        def _():
            own_input(m).wait()

        for k in range(PARTS):
            @pl.when(s > 0)
            def _():
                for p in needs[k]:
                    if p != middle:
                        forward_piece(m, p, halo).wait_recv()

            if k == last_part:
                forward_piece(m, middle, halo).wait_recv()
            fresh = pl.ds(run_start(*fresh_runs[k]) + 1, fresh_runs[k][1])
            left, right = column_shifts(x3[m, fresh, :, mid].astype(jnp.float32))
            x3[m, fresh, :, pl.ds(0, chans)] = left
            x3[m, fresh, :, pl.ds(2 * chans, chans)] = right
            start = run_start(k * step, step)
            pre = conv(x3.at[m], w_ref, start)
            curved = jnp.tanh(tanh_scale * (pre + cubic_term * pre * pre * pre))
            value = 0.5 * pre * (1.0 + curved)
            out_ref[m, pl.ds(start, step)] = value.astype(jnp.bfloat16).reshape(step, cols, chans)

            @pl.when(s < last)
            def _():
                for p in gives[k]:
                    forward_piece(m, p, other_halo).start()

            steep = 0.5 * (1.0 + curved) + 0.5 * pre * (1.0 - curved * curved) * tanh_scale * (
                1.0 + 3.0 * cubic_term * pre * pre
            )
            slope[m, pl.ds(start + 1, step)] = steep.reshape(step, cols, chans)
        slope_halo(m, other_halo).start()

    def kernel_term(m, a):
        return lax.dot_general(
            x3[m, pl.ds(a, rows)].reshape(rows * cols, 3 * chans),
            g3[pl.ds(1, rows), :, mid].reshape(rows * cols, chans),
            (((0,), (0,)), ((), ())),
            preferred_element_type=jnp.float32,
        )

    def backward(m):
        @pl.when(is_last)
        def _():
            own_cotangent(m).wait()

        for k in range(PARTS):
            @pl.when(s < last)
            def _():
                for p in needs[k]:
                    if p != middle:
                        backward_piece(m, p, halo).wait_recv()

            if k == last_part:
                backward_piece(m, middle, halo).wait_recv()
                slope_halo(m, halo).wait_recv()
            fresh = pl.ds(run_start(*fresh_runs[k]) + 1, fresh_runs[k][1])
            local = (u[m, fresh].astype(jnp.float32) * slope[m, fresh]).astype(jnp.bfloat16)
            left, right = column_shifts(local.astype(jnp.float32))
            g3[fresh, :, pl.ds(0, chans)] = left
            g3[fresh, :, mid] = local
            g3[fresh, :, pl.ds(2 * chans, chans)] = right
            start = run_start(k * step, step)
            passed = conv(g3, wt, start)
            grad_ref[m, pl.ds(start, step)] = passed.astype(jnp.bfloat16).reshape(step, cols, chans)

            @pl.when(s > 0)
            def _():
                for p in gives[k]:
                    backward_piece(m, p, other_halo).start()

        @pl.when(m == 0)
        def _():
            for a in range(3):
                acc[pl.ds(a * 3 * chans, 3 * chans), :] = kernel_term(m, a)

        @pl.when(jnp.logical_and(m > 0, m < micros - 1))
        def _():
            for a in range(3):
                acc[pl.ds(a * 3 * chans, 3 * chans), :] += kernel_term(m, a)

    def forward_step(m, carry):
        forward(m)

        @pl.when(is_last)
        def _():
            backward(m)

        return carry

    lax.fori_loop(0, micros, forward_step, 0)

    @pl.when(s == 0)
    def _():
        transpose_weights()

    def backward_step(m, carry):
        backward(m)
        return carry

    @pl.when(s < last)
    def _():
        lax.fori_loop(0, micros, backward_step, 0)

    def kernel_copy(a):
        block = pl.ds(a * 3 * chans, 3 * chans)
        return pltpu.make_async_remote_copy(
            src_ref=wsend.at[block],
            dst_ref=wrecv.at[block],
            send_sem=send_w.at[a],
            recv_sem=recv_w.at[a],
            device_id={"rows": other},
            device_id_type=MESH,
        )

    for a in range(3):
        block = pl.ds(a * 3 * chans, 3 * chans)
        term = kernel_term(micros - 1, a)
        total = term if micros == 1 else acc[block, :] + term
        wsend[block, :] = total.astype(jnp.bfloat16)
        kernel_copy(a).start()
    for a in range(3):
        block = pl.ds(a * 3 * chans, 3 * chans)
        kernel_copy(a).wait_recv()
        wgrad_ref[block, :] = (
            wsend[block, :].astype(jnp.float32) + wrecv[block, :].astype(jnp.float32)
        ) * factor

    def finish(m, carry):
        slope_halo(m, other_halo).wait_send()

        @pl.when(s < last)
        def _():
            for p in range(2 * PARTS):
                forward_piece(m, p, other_halo).wait_send()

        @pl.when(s > 0)
        def _():
            for p in range(2 * PARTS):
                backward_piece(m, p, other_halo).wait_send()

        @pl.when(is_first)
        def _():
            first_halo(m, other_halo).wait_send()

        @pl.when(is_last)
        def _():
            last_halo(m, other_halo).wait_send()

        return carry

    lax.fori_loop(0, micros, finish, 0)
    for a in range(3):
        kernel_copy(a).wait_send()


def on_device(inputs, weights, cotangent):
    micros, rows, cols, chans = inputs.shape
    depth = weights.shape[1]
    section_count = lax.axis_size("section")
    factor = 1.0 / math.sqrt(micros * rows * lax.axis_size("rows") * cols)
    vmem = pl.BlockSpec(memory_space=pltpu.VMEM)
    dma = pltpu.SemaphoreType.DMA
    bf16, f32 = jnp.bfloat16, jnp.float32
    outs = pl.pallas_call(
        functools.partial(kernel, section_count, factor),
        out_shape=(
            jax.ShapeDtypeStruct((micros, rows, cols, chans), bf16),
            jax.ShapeDtypeStruct((micros, rows, cols, chans), bf16),
            jax.ShapeDtypeStruct((depth, chans), f32),
        ),
        in_specs=[pl.BlockSpec(memory_space=pl.ANY)] * 3,
        out_specs=(vmem,) * 3,
        scratch_shapes=[
            pltpu.VMEM((depth, chans), bf16),
            pltpu.VMEM((micros, rows + 2, cols, 3 * chans), bf16),
            pltpu.VMEM((micros, rows + 2, cols, chans), bf16),
            pltpu.VMEM((micros, rows + 2, cols, chans), f32),
            pltpu.VMEM((rows + 2, cols, 3 * chans), bf16),
            pltpu.VMEM((depth, chans), bf16),
            pltpu.VMEM((depth, chans), f32),
            pltpu.VMEM((depth, chans), bf16),
            pltpu.VMEM((depth, chans), bf16),
            dma((micros, 2 * PARTS)),
            dma((micros, 2 * PARTS)),
            dma((micros, 2 * PARTS)),
            dma((micros, 2 * PARTS)),
            dma((micros,)),
            dma((micros,)),
            dma((micros,)),
            dma((micros,)),
            dma((3,)),
            dma((3,)),
            dma((micros,)),
            dma,
        ],
        compiler_params=pltpu.CompilerParams(
            collective_id=0, has_side_effects=True, vmem_limit_bytes=48 * 1024 * 1024
        ),
        name="relay",
    )(inputs, weights[0], cotangent)
    section_outputs, grad_inputs, weight_grads = outs
    return (section_outputs[None], grad_inputs[None], weight_grads[None])


def solution(mesh):
    placed = (
        P("groups", "rows", None, None),
        P("section", None, None),
        P("groups", "rows", None, None),
    )
    return jax.shard_map(
        on_device,
        mesh=mesh,
        in_specs=placed,
        out_specs=(
            P("section", "groups", "rows", None, None),
            P("section", "groups", "rows", None, None),
            P("section", "groups", None),
        ),
        check_vma=False,
    )
```

```python
import functools
import math

import jax
import jax.numpy as jnp
from jax import lax
from jax.experimental import pallas as pl
from jax.experimental.pallas import tpu as pltpu
from jax.sharding import PartitionSpec as P

MESH = pl.DeviceIdType.MESH
tanh_scale = 0.7978845608028654
cubic_term = 0.044715
PARTS = 4


def column_shifts(values):
    rows, cols, channels = values.shape
    flat = values.reshape(rows * cols, channels)
    col = lax.broadcasted_iota(jnp.int32, flat.shape, 0) % cols
    left = jnp.where(col == 0, 0.0, pltpu.roll(flat, 1, 0))
    right = jnp.where(col == cols - 1, 0.0, pltpu.roll(flat, rows * cols - 1, 0))
    return (
        left.astype(jnp.bfloat16).reshape(values.shape),
        right.astype(jnp.bfloat16).reshape(values.shape),
    )


def kernel(
    section_count,
    in_ref,
    w_hbm,
    cot_ref,
    out_ref,
    grad_ref,
    wsend,
    wrecv,
    w_ref,
    x3,
    u,
    slope,
    g3,
    wt,
    acc,
    send_f,
    recv_f,
    send_b,
    recv_b,
    send_i,
    send_c,
    send_s,
    recv_s,
    send_w,
    recv_w,
    sem_in,
    sem_wt,
):
    micros, rows, cols, chans = in_ref.shape
    step = rows // PARTS
    last_part = PARTS - 1
    mid = pl.ds(chans, chans)
    s = lax.axis_index("section")
    r = lax.axis_index("rows")
    other = 1 - r
    last = section_count - 1
    is_first = s == 0
    is_last = s == last

    edge = (1 - r) * (rows - 1)
    halo = (1 - r) * (rows + 1)
    other_halo = r * (rows + 1)

    weight_copy = pltpu.make_async_copy(w_hbm, w_ref, sem_wt)
    weight_copy.start()

    def own_input(m):
        return pltpu.make_async_copy(in_ref.at[m], x3.at[m, pl.ds(1, rows), :, mid], sem_in.at[m])

    def own_cotangent(m):
        return pltpu.make_async_copy(cot_ref.at[m], u.at[m, pl.ds(1, rows)], sem_in.at[m])

    def each_micro(action):
        def body(m, carry):
            action(m)
            return carry

        lax.fori_loop(0, micros, body, 0)

    @pl.when(is_first)
    def _():
        each_micro(lambda m: own_input(m).start())

    @pl.when(is_last)
    def _():
        each_micro(lambda m: own_cotangent(m).start())

    barrier = pltpu.get_barrier_semaphore()
    pl.semaphore_signal(barrier, inc=1, device_id={"rows": other}, device_id_type=MESH)

    @pl.when(s > 0)
    def _():
        for core in range(2):
            pl.semaphore_signal(
                barrier, inc=1, device_id={"section": s - 1, "rows": core}, device_id_type=MESH
            )

    @pl.when(s < last)
    def _():
        for core in range(2):
            pl.semaphore_signal(
                barrier, inc=1, device_id={"section": s + 1, "rows": core}, device_id_type=MESH
            )

    peers = 1 + 2 * (s > 0).astype(jnp.int32) + 2 * (s < last).astype(jnp.int32)
    pl.semaphore_wait(barrier, peers)

    def first_halo(m, dst_row):
        return pltpu.make_async_remote_copy(
            src_ref=in_ref.at[m, pl.ds(edge, 1)],
            dst_ref=x3.at[m, pl.ds(dst_row, 1), :, mid],
            send_sem=send_i.at[m],
            recv_sem=recv_f.at[m, 2 * PARTS - 1],
            device_id={"rows": other},
            device_id_type=MESH,
        )

    def last_halo(m, dst_row):
        return pltpu.make_async_remote_copy(
            src_ref=cot_ref.at[m, pl.ds(edge, 1)],
            dst_ref=u.at[m, pl.ds(dst_row, 1)],
            send_sem=send_c.at[m],
            recv_sem=recv_b.at[m, 2 * PARTS - 1],
            device_id={"rows": other},
            device_id_type=MESH,
        )

    def slope_halo(m, dst_row):
        return pltpu.make_async_remote_copy(
            src_ref=slope.at[m, pl.ds(edge + 1, 1)],
            dst_ref=slope.at[m, pl.ds(dst_row, 1)],
            send_sem=send_s.at[m],
            recv_sem=recv_s.at[m],
            device_id={"rows": other},
            device_id_type=MESH,
        )

    def run_start(q, n):
        return q + r * (rows - 2 * q - n)

    pieces = [(0, step)]
    pieces += [(k * step + 1, step - 1) for k in range(1, PARTS)]
    pieces += [(k * step, 1) for k in range(1, PARTS)]
    pieces += [(rows - 1, 1)]
    middle = 2 * PARTS - 1
    needs = [(k, PARTS + k if k < last_part else middle) for k in range(PARTS)]
    gives = [(0,)] + [(PARTS - 1 + k, k) for k in range(1, last_part)]
    gives += [(PARTS - 1 + last_part, middle, last_part)]

    def forward_piece(m, p, halo_row):
        q, count = pieces[p]
        start = run_start(q, count)
        where = halo_row if p == middle else start + 1
        return pltpu.make_async_remote_copy(
            src_ref=out_ref.at[m, pl.ds(start, count)],
            dst_ref=x3.at[m, pl.ds(where, count), :, mid],
            send_sem=send_f.at[m, p],
            recv_sem=recv_f.at[m, p],
            device_id={"section": jnp.minimum(s + 1, last), "rows": other if p == middle else r},
            device_id_type=MESH,
        )

    def backward_piece(m, p, halo_row):
        q, count = pieces[p]
        start = run_start(q, count)
        where = halo_row if p == middle else start + 1
        return pltpu.make_async_remote_copy(
            src_ref=grad_ref.at[m, pl.ds(start, count)],
            dst_ref=u.at[m, pl.ds(where, count)],
            send_sem=send_b.at[m, p],
            recv_sem=recv_b.at[m, p],
            device_id={"section": jnp.maximum(s - 1, 0), "rows": other if p == middle else r},
            device_id_type=MESH,
        )

    @pl.when(is_first)
    def _():
        each_micro(lambda m: first_halo(m, other_halo).start())

    @pl.when(is_last)
    def _():
        each_micro(lambda m: last_halo(m, other_halo).start())

    blank = jnp.zeros((1, cols, 3 * chans), jnp.bfloat16)

    def clear(m, carry):
        x3[m, pl.ds(other_halo, 1)] = blank
        return carry

    lax.fori_loop(0, micros, clear, 0)
    g3[pl.ds(other_halo, 1)] = blank

    weight_copy.wait()

    def transpose_weights():
        for k in range(9):
            wt[pl.ds((8 - k) * chans, chans), :] = w_ref[pl.ds(k * chans, chans), :].T

    @pl.when(s > 0)
    def _():
        transpose_weights()

    fresh_runs = [(0, step + 1)] + [(k * step + 1, step) for k in range(1, PARTS)]

    def conv(field, kern, start):
        total = None
        for a in range(3):
            part = jnp.dot(
                field[pl.ds(start + a, step)].reshape(step * cols, 3 * chans),
                kern[pl.ds(a * 3 * chans, 3 * chans), :],
                preferred_element_type=jnp.float32,
            )
            total = part if total is None else total + part
        return total

    def forward(m):
        @pl.when(is_first)
        def _():
            own_input(m).wait()

        for k in range(PARTS):
            @pl.when(s > 0)
            def _():
                for p in needs[k]:
                    if p != middle:
                        forward_piece(m, p, halo).wait_recv()

            if k == last_part:
                forward_piece(m, middle, halo).wait_recv()
            fresh = pl.ds(run_start(*fresh_runs[k]) + 1, fresh_runs[k][1])
            left, right = column_shifts(x3[m, fresh, :, mid].astype(jnp.float32))
            x3[m, fresh, :, pl.ds(0, chans)] = left
            x3[m, fresh, :, pl.ds(2 * chans, chans)] = right
            start = run_start(k * step, step)
            pre = conv(x3.at[m], w_ref, start)
            curved = jnp.tanh(tanh_scale * (pre + cubic_term * pre * pre * pre))
            value = 0.5 * pre * (1.0 + curved)
            out_ref[m, pl.ds(start, step)] = value.astype(jnp.bfloat16).reshape(step, cols, chans)

            @pl.when(s < last)
            def _():
                for p in gives[k]:
                    forward_piece(m, p, other_halo).start()

            steep = 0.5 * (1.0 + curved) + 0.5 * pre * (1.0 - curved * curved) * tanh_scale * (
                1.0 + 3.0 * cubic_term * pre * pre
            )
            slope[m, pl.ds(start + 1, step)] = steep.reshape(step, cols, chans)
        slope_halo(m, other_halo).start()

    def kernel_term(m, a):
        return lax.dot_general(
            x3[m, pl.ds(a, rows)].reshape(rows * cols, 3 * chans),
            g3[pl.ds(1, rows), :, mid].reshape(rows * cols, chans),
            (((0,), (0,)), ((), ())),
            preferred_element_type=jnp.float32,
        )

    def backward(m):
        @pl.when(is_last)
        def _():
            own_cotangent(m).wait()

        for k in range(PARTS):
            @pl.when(s < last)
            def _():
                for p in needs[k]:
                    if p != middle:
                        backward_piece(m, p, halo).wait_recv()

            if k == last_part:
                backward_piece(m, middle, halo).wait_recv()
                slope_halo(m, halo).wait_recv()
            fresh = pl.ds(run_start(*fresh_runs[k]) + 1, fresh_runs[k][1])
            local = (u[m, fresh].astype(jnp.float32) * slope[m, fresh]).astype(jnp.bfloat16)
            left, right = column_shifts(local.astype(jnp.float32))
            g3[fresh, :, pl.ds(0, chans)] = left
            g3[fresh, :, mid] = local
            g3[fresh, :, pl.ds(2 * chans, chans)] = right
            start = run_start(k * step, step)
            passed = conv(g3, wt, start)
            grad_ref[m, pl.ds(start, step)] = passed.astype(jnp.bfloat16).reshape(step, cols, chans)

            @pl.when(s > 0)
            def _():
                for p in gives[k]:
                    backward_piece(m, p, other_halo).start()

        @pl.when(m == 0)
        def _():
            for a in range(3):
                acc[pl.ds(a * 3 * chans, 3 * chans), :] = kernel_term(m, a)

        @pl.when(jnp.logical_and(m > 0, m < micros - 1))
        def _():
            for a in range(3):
                acc[pl.ds(a * 3 * chans, 3 * chans), :] += kernel_term(m, a)

    def forward_step(m, carry):
        forward(m)

        @pl.when(is_last)
        def _():
            backward(m)

        return carry

    lax.fori_loop(0, micros, forward_step, 0)

    @pl.when(s == 0)
    def _():
        transpose_weights()

    def backward_step(m, carry):
        backward(m)
        return carry

    @pl.when(s < last)
    def _():
        lax.fori_loop(0, micros, backward_step, 0)

    def kernel_copy(a):
        block = pl.ds(a * 3 * chans, 3 * chans)
        return pltpu.make_async_remote_copy(
            src_ref=wsend.at[block],
            dst_ref=wrecv.at[block],
            send_sem=send_w.at[a],
            recv_sem=recv_w.at[a],
            device_id={"rows": other},
            device_id_type=MESH,
        )

    for a in range(3):
        block = pl.ds(a * 3 * chans, 3 * chans)
        term = kernel_term(micros - 1, a)
        total = term if micros == 1 else acc[block, :] + term
        wsend[block, :] = total.astype(jnp.bfloat16)
        kernel_copy(a).start()
    for a in range(3):
        kernel_copy(a).wait_recv()

    def finish(m, carry):
        slope_halo(m, other_halo).wait_send()

        @pl.when(s < last)
        def _():
            for p in range(2 * PARTS):
                forward_piece(m, p, other_halo).wait_send()

        @pl.when(s > 0)
        def _():
            for p in range(2 * PARTS):
                backward_piece(m, p, other_halo).wait_send()

        @pl.when(is_first)
        def _():
            first_halo(m, other_halo).wait_send()

        @pl.when(is_last)
        def _():
            last_halo(m, other_halo).wait_send()

        return carry

    lax.fori_loop(0, micros, finish, 0)
    for a in range(3):
        kernel_copy(a).wait_send()


def on_device(inputs, weights, cotangent):
    micros, rows, cols, chans = inputs.shape
    depth = weights.shape[1]
    section_count = lax.axis_size("section")
    factor = 1.0 / math.sqrt(micros * rows * lax.axis_size("rows") * cols)
    vmem = pl.BlockSpec(memory_space=pltpu.VMEM)
    dma = pltpu.SemaphoreType.DMA
    bf16, f32 = jnp.bfloat16, jnp.float32
    outs = pl.pallas_call(
        functools.partial(kernel, section_count),
        out_shape=(
            jax.ShapeDtypeStruct((micros, rows, cols, chans), bf16),
            jax.ShapeDtypeStruct((micros, rows, cols, chans), bf16),
            jax.ShapeDtypeStruct((depth, chans), bf16),
            jax.ShapeDtypeStruct((depth, chans), bf16),
        ),
        in_specs=[pl.BlockSpec(memory_space=pl.ANY)] * 3,
        out_specs=(vmem,) * 4,
        scratch_shapes=[
            pltpu.VMEM((depth, chans), bf16),
            pltpu.VMEM((micros, rows + 2, cols, 3 * chans), bf16),
            pltpu.VMEM((micros, rows + 2, cols, chans), bf16),
            pltpu.VMEM((micros, rows + 2, cols, chans), f32),
            pltpu.VMEM((rows + 2, cols, 3 * chans), bf16),
            pltpu.VMEM((depth, chans), bf16),
            pltpu.VMEM((depth, chans), f32),
            dma((micros, 2 * PARTS)),
            dma((micros, 2 * PARTS)),
            dma((micros, 2 * PARTS)),
            dma((micros, 2 * PARTS)),
            dma((micros,)),
            dma((micros,)),
            dma((micros,)),
            dma((micros,)),
            dma((3,)),
            dma((3,)),
            dma((micros,)),
            dma,
        ],
        compiler_params=pltpu.CompilerParams(
            collective_id=0, has_side_effects=True, vmem_limit_bytes=48 * 1024 * 1024
        ),
        name="relay",
    )(inputs, weights[0], cotangent)
    section_outputs, grad_inputs, mine, theirs = outs
    weight_grads = (mine.astype(f32) + theirs.astype(f32)) * factor
    return (section_outputs[None], grad_inputs[None], weight_grads[None])


def solution(mesh):
    placed = (
        P("groups", "rows", None, None),
        P("section", None, None),
        P("groups", "rows", None, None),
    )
    return jax.shard_map(
        on_device,
        mesh=mesh,
        in_specs=placed,
        out_specs=(
            P("section", "groups", "rows", None, None),
            P("section", "groups", "rows", None, None),
            P("section", "groups", None),
        ),
        check_vma=False,
    )
```
